128 devices in a mesh: win: 4 (over x), chan: 32 (over y, z, core).
Axes of the slice: x: 4, y: 4, z: 4, core: 2. Of those that a mesh axis runs over, the one named last changes fastest.
Arguments:
- traces: bfloat16 [2048, 16, 14976], P('chan', 'win'), may hold values from -100 to 100
- fetch_rows: int32 [32, 32, 8], replicated, may hold values from 0 to 63, as said below
- pair_slots: int32 [512, 2, 128], P('chan'), may hold values from 0 to 255, as said below
- tile_count: int32 [32], P('chan'), may hold values from 1 to 16, 256 in all
Outputs:
- stacks: float32 [512, 128, 2001], P('chan', 'win')
The draws below stay inside these ranges and needn't reach their ends.
Inputs may be any that keep to these rules, and one draw needn't show every extreme that they name: `fetch_rows`: the 8 entries of one owner and one block are distinct channels of that block. `pair_slots`: the source and receiver entries of a pair differ. `tile_count`: the counts of all owners add up to 256.
All inputs are finite; a program needn't handle non-finite values. No bound on the sum of `tile_count` on one device may be relied on, other than what follows from the above.
Results may differ from the reference program's by a relative error of at most 0.0094.
Values may be sent and summed in bfloat16 or wider, within the bound.
A program may use at most 128 MiB of HBM per device.

```python
import math
import jax
import jax.numpy as jnp
import numpy as np
from jax import lax

CH_DEV = 64
TSLOT = 16
S = 14976
FREQS = 512
SMOOTH = 64
LOW_BIN = 60
PT = 128
CAP = 8
MAXLAG = 1000
CHANNELS = 2048
WINDOWS = 16
TILES = 512
TABLE = 256
LAGS = 2001
N_CHAN = 32


def draw_traces(key, part):
    key = jax.random.fold_in(key, 7)
    k_noise, k_scale, k_memory = jax.random.split(key, 3)
    full_shape = (CHANNELS, WINDOWS, S + 1)
    white_noise = jnp.clip(jax.random.normal(k_noise, full_shape, jnp.float32), -5.0, 5.0)
    gain_top = 10.0
    channel_gain = jnp.exp(jax.random.uniform(k_scale, (CHANNELS, WINDOWS, 1), jnp.float32, 0.0, math.log(gain_top)))
    memory_coef = jax.random.uniform(k_memory, (CHANNELS, 1, 1), jnp.float32, -0.99, -0.85)
    return (channel_gain * (white_noise[:, :, 1:] + memory_coef * white_noise[:, :, :-1])).astype(jnp.bfloat16)


def draw_fetch_rows(key, part):
    key = jax.random.fold_in(key, 21)
    scores = jax.random.randint(key, (N_CHAN, N_CHAN, CH_DEV), 0, 1 << 20) * CH_DEV
    scores = scores + lax.broadcasted_iota(jnp.int32, (N_CHAN, N_CHAN, CH_DEV), 2)
    return lax.top_k(scores, CAP)[1].astype(jnp.int32)


def draw_pair_slots(key, part):
    key = jax.random.fold_in(key, 33)
    k_src, k_exp, k_off = jax.random.split(key, 3)
    source = jax.random.randint(k_src, (TILES, PT), 0, TABLE)
    exponent = jax.random.randint(k_exp, (TILES, PT), 0, 9)
    spread_max = jnp.left_shift(jnp.ones_like(exponent), exponent)
    offset = 1 + jax.random.randint(k_off, (TILES, PT), 0, spread_max) % (TABLE - 1)
    receiver = (source + offset) % TABLE
    return jnp.stack([source, receiver], axis=1).astype(jnp.int32)


def length_profile(number_of, total, limit, slope):
    portions = [(1 << 20) // math.isqrt(standing ** slope) + 1 for standing in range(2, number_of + 1)]
    rest, counts = total - limit - (number_of - 1), [1] * (number_of - 1)
    while rest > 0:
        candidates = [i for i in range(number_of - 1) if counts[i] < limit]
        whole, budget = sum([portions[i] for i in candidates]), rest
        for i in candidates:
            more = min(limit - counts[i], max(1, budget * portions[i] // whole), rest)
            counts[i] = counts[i] + more
            rest = rest - more
    return np.array([limit] + counts)


def ragged_sizes(stream_key, number_of, total, most, slope):
    if number_of == 2:
        one = jax.random.randint(stream_key, (), max(1, total - most), min(most, total - 1) + 1)
        return jnp.stack([one, total - one])
    lengths = jnp.asarray(length_profile(number_of, total, most, slope), jnp.int32)
    twos = (number_of - 1) // 2
    donor, taker = lengths[1:1 + 2 * twos:2], lengths[2:2 + 2 * twos:2]
    room = jnp.minimum(donor - 1, most - taker)
    shifted = jax.random.randint(jax.random.fold_in(stream_key, 1), (twos,), 0, 1 << 20) % (room + 1)
    lengths = lengths.at[1:1 + 2 * twos:2].set(donor - shifted).at[2:2 + 2 * twos:2].set(taker + shifted)
    return lengths[jax.random.permutation(jax.random.fold_in(stream_key, 2), number_of)]


def setup_inputs(seed: int = 0) -> dict:
    seeds = jax.random.split(jax.random.key(seed), 5)
    return {
        "traces": draw_traces(jax.random.fold_in(seeds[4], 71), 0),
        "fetch_rows": draw_fetch_rows(jax.random.fold_in(seeds[4], 71), 0),
        "pair_slots": draw_pair_slots(jax.random.fold_in(seeds[4], 71), 0),
        "tile_count": ragged_sizes(seeds[3], N_CHAN, TILES // 2, TSLOT, 2).astype(jnp.int32),
    }


def band_table(length, first_bin, band_bins):
    samples = lax.broadcasted_iota(jnp.int32, (length, band_bins), 0)
    bin_index = lax.broadcasted_iota(jnp.int32, (length, band_bins), 1) + first_bin
    phase_index = samples * bin_index % length
    angles = phase_index.astype(jnp.float32) * (2.0 * math.pi / length)
    return jnp.concatenate([jnp.cos(angles), -jnp.sin(angles)], axis=1)

def lag_table(length, first_bin, band_bins, max_lag, lag_scale):
    lag_count = 2 * max_lag + 1
    bin_index = lax.broadcasted_iota(jnp.int32, (band_bins, lag_count), 0) + first_bin
    lag_index = lax.broadcasted_iota(jnp.int32, (band_bins, lag_count), 1) - max_lag + length
    phase_index = bin_index * lag_index % length
    angles = phase_index.astype(jnp.float32) * (2.0 * math.pi / length)
    return jnp.concatenate([jnp.cos(angles) * lag_scale, -jnp.sin(angles) * lag_scale], axis=0)

def whiten(spectra, band_bins, smooth_bins):
    real_part = spectra[:, :band_bins]
    imag_part = spectra[:, band_bins:]
    magnitude = jnp.sqrt(real_part * real_part + imag_part * imag_part)
    level_mean = lax.optimization_barrier(jnp.mean(magnitude.reshape(magnitude.shape[0], band_bins // smooth_bins, smooth_bins), axis=2))
    level_full = jnp.repeat(level_mean, smooth_bins, axis=1) + 1e-06
    return jnp.concatenate([real_part / level_full, imag_part / level_full], axis=1).astype(jnp.bfloat16)

def cross_spectra(channel_table, tile_slots, band_bins):
    source_rows = jnp.take(channel_table, tile_slots[:, 0, :], axis=0).astype(jnp.float32)
    receiver_rows = jnp.take(channel_table, tile_slots[:, 1, :], axis=0).astype(jnp.float32)
    source_re = source_rows[..., :band_bins]
    source_im = source_rows[..., band_bins:]
    receiver_re = receiver_rows[..., :band_bins]
    receiver_im = receiver_rows[..., band_bins:]
    real_part = lax.optimization_barrier(jnp.sum(source_re * receiver_re + source_im * receiver_im, axis=2))
    imag_part = lax.optimization_barrier(jnp.sum(source_im * receiver_re - source_re * receiver_im, axis=2))
    return jnp.concatenate([real_part, imag_part], axis=-1)

def reference(traces, fetch_rows, pair_slots, tile_count):
    dft_table = band_table(S, LOW_BIN, FREQS).astype(jnp.bfloat16)

    def spectra_of(trace_block):
        flat_rows = trace_block.reshape(CH_DEV * WINDOWS, S)
        spectra = jnp.dot(flat_rows, dft_table, preferred_element_type=jnp.float32)
        return whiten(spectra, FREQS, SMOOTH).reshape(CH_DEV, WINDOWS, 2 * FREQS)
    whitened = lax.map(spectra_of, traces.reshape(N_CHAN, CH_DEV, WINDOWS, S))
    whitened = whitened.reshape(CHANNELS, WINDOWS, 2 * FREQS)
    inverse = lag_table(S, LOW_BIN, FREQS, MAXLAG, 1.0 / math.sqrt(FREQS * WINDOWS))
    offsets = jnp.arange(N_CHAN, dtype=jnp.int32)[:, None] * CH_DEV

    def owner_stacks(owner_index):
        listed = (fetch_rows[owner_index] + offsets).reshape(-1).astype(jnp.int32)
        channel_table = jnp.take(whitened, listed, axis=0)
        tile_slots = lax.dynamic_slice_in_dim(pair_slots, (owner_index * TSLOT).astype(jnp.int32), TSLOT, 0)
        cross = cross_spectra(channel_table, tile_slots, FREQS)
        live_tiles = jnp.arange(TSLOT, dtype=jnp.int32) < tile_count[owner_index]
        cross = jnp.where(live_tiles[:, None, None], cross, jnp.zeros_like(cross))
        lagged = jnp.dot(cross.reshape(TSLOT * PT, 2 * FREQS), inverse, precision=lax.Precision.HIGHEST, preferred_element_type=jnp.float32)
        return lagged.reshape(TSLOT, PT, LAGS)
    stacks = lax.map(owner_stacks, jnp.arange(N_CHAN, dtype=jnp.int32))
    return stacks.reshape(TILES, PT, LAGS)
```

```python
import functools
import math

import jax
import jax.numpy as jnp
import ml_dtypes
import numpy as np
from jax import lax
from jax.experimental import pallas as pl
from jax.experimental.pallas import tpu as pltpu
from jax.sharding import PartitionSpec as P

MESH=pl.DeviceIdType.MESH
S=14976
def quarter_table():
    s=np.arange(3840)[:,None]; k=np.arange(512)[None]+60
    a=((s*k)%S)*(2*math.pi/S)
    c=np.cos(a).reshape(3840,8,1,64); d=-np.sin(a).reshape(3840,8,1,64)
    return np.concatenate([c,d],2).reshape(3840,1024).astype(ml_dtypes.bfloat16)
def turn_rows():
    lane=np.arange(1024)%128; k=(np.arange(1024)//128)*64+lane%64; im=lane>=64
    s=np.where(k%2==0,1.,-1.)
    al=np.array([1,0,-1,0.])[k%4]
    be=np.where(im,np.array([0,-1,0,1.])[k%4],np.array([0,1,0,-1.])[k%4])
    return np.stack([s,al,be]+[s*0]*5).astype(np.float32)
FIRST=(0,30,59,88); COUNT=(30,29,29,29); SHIFT=(0,96,64,32)
CUT=15
def k1(x_ref,t_ref,r_ref,o_ref,xs,ts,acc,xsem,tsem):
    tp=[(0,1920+96),(2016,3840-2016)]
    tc=[pltpu.make_async_copy(t_ref.at[pl.ds(a,n)],ts.at[pl.ds(a,n)],tsem.at[i]) for i,(a,n) in enumerate(tp)]
    def xpiece(q,i):
        a=128*(FIRST[q]+(CUT if i else 0)); n=128*(COUNT[q]-CUT if i else CUT)
        return a,n
    xc={}
    for i in range(2):
        for q in range(4):
            a,n=xpiece(q,i)
            xc[q,i]=pltpu.make_async_copy(x_ref.at[:,:,pl.ds(a,n)],xs.at[:,:,pl.ds(a,n)],xsem.at[q,i])
    tc[0].start(); xc[0,0].start(); xc[1,0].start(); xc[2,0].start(); xc[3,0].start()
    tc[1].start()
    for q in range(4): xc[q,1].start()
    for i in range(2):
        tc[i].wait()
        for q in range(4):
            xc[q,i].wait()
            a,n=xpiece(q,i)
            x=xs[:,:,a:a+n].reshape(256,n)
            r0=SHIFT[q]+(128*CUT if i else 0)
            for j in range(4):
                cs=slice(256*j,256*j+256)
                y=jnp.dot(x,ts[r0:r0+n,cs],preferred_element_type=jnp.float32)
                acc[q,:,cs]=y if i==0 else acc[q,:,cs]+y
    for b in range(8):
        cs=slice(128*b,128*b+128)
        s,al,be=r_ref[0:1,cs],r_ref[1:2,cs],r_ref[2:3,cs]
        g0,g1,g2,g3=(acc[q,:,cs] for q in range(4))
        z=g0+s*g2+al*(g1+g3)+be*pltpu.roll(g1-g3,64,1)
        sq=z*z
        mag=jnp.sqrt(sq+pltpu.roll(sq,64,1))
        lev=jnp.sum(mag,axis=1,keepdims=True)*(1/128)+1e-6
        o_ref[b]=(z/lev).astype(jnp.bfloat16)
def dft(x,tab,turn):
    return pl.pallas_call(k1,out_shape=jax.ShapeDtypeStruct((8,256,128),jnp.bfloat16),
      in_specs=[pl.BlockSpec(memory_space=pl.ANY),pl.BlockSpec(memory_space=pl.ANY),pl.BlockSpec(memory_space=pltpu.VMEM)],
      out_specs=pl.BlockSpec(memory_space=pltpu.VMEM),
      scratch_shapes=[pltpu.VMEM((64,4,14976),jnp.bfloat16),pltpu.VMEM((3840,1024),jnp.bfloat16),pltpu.VMEM((4,256,1024),jnp.float32),
        pltpu.SemaphoreType.DMA((4,2)),pltpu.SemaphoreType.DMA((2,))],
      compiler_params=pltpu.CompilerParams(vmem_limit_bytes=56<<20))(x,tab,turn)
G=32
def k3(slots,count,t_ref,o_ref,a1,a2,r1,r2,sr):
    lane=lax.broadcasted_iota(jnp.int32,(1,1,128),2)
    sign=jnp.where(lane<64,1.0,-1.0).astype(jnp.float32)
    low=lax.broadcasted_iota(jnp.int32,(G,128),1)<64
    ri=lax.broadcasted_iota(jnp.int32,(256,256),0); ci=lax.broadcasted_iota(jnp.int32,(256,256),1); cl=ci%128
    one=lambda m,v: jnp.where(m,v,0.0).astype(jnp.bfloat16)
    perm=jnp.concatenate([one(ri==ci+jnp.where(cl<64,64,-64),jnp.where(cl<64,1.0,-1.0)),one(ri==ci-jnp.where(cl<64,0,64),1.0),one(ri==ci+jnp.where(cl<64,64,0),1.0)],1)
    def prep(i,_):
        rows=pl.ds(i*16,16)
        x=jnp.concatenate([t_ref[0,rows].reshape(256,128),t_ref[1,rows].reshape(256,128)],1)
        y=jnp.dot(x,perm,preferred_element_type=jnp.float32)
        for h in range(2):
            a1[rows,h]=t_ref[h,rows].astype(a1.dtype)
            for m,ref in enumerate((a2,r1,r2)):
                ref[rows,h]=y[:,256*m+128*h:256*m+128*h+128].reshape(16,16,128).astype(ref.dtype)
        return 0
    lax.fori_loop(0,16,prep,0)
    def tile(t,_):
        @pl.when(t<count[0])
        def _live():
            def reduce(w):
                for h in range(2):
                    v=[sr[w,h,pl.ds(j,G,stride=8)] for j in range(8)]
                    x=((v[0]+v[1])+(v[2]+v[3]))+((v[4]+v[5])+(v[6]+v[7]))
                    o_ref[h,w,pl.ds(pl.multiple_of(t*32,32),32)]=x.astype(jnp.bfloat16)
            for w in range(4):
                for i in range(G):
                    s=slots[t*256+w*G+i]; r=slots[t*256+128+w*G+i]
                    for h in range(2):
                        q=a1[s,h]*r1[r,h]+a2[s,h]*r2[r,h]
                        sr[w,h,pl.ds(8*i,8)]=q[:8]+q[8:]
                if w: reduce(w-1)
            reduce(3)
        @pl.when(t>=count[0])
        def _dead():
            for h in range(2):
                for w in range(4):
                    o_ref[h,w,pl.ds(pl.multiple_of(t*32,32),32)]=jnp.zeros((32,128),jnp.bfloat16)
        return 0
    lax.fori_loop(0,16,tile,0)
def cross(slots,count,tab):
    return pl.pallas_call(k3,out_shape=jax.ShapeDtypeStruct((2,4,512,128),jnp.bfloat16),
      in_specs=[pl.BlockSpec(memory_space=pltpu.SMEM),pl.BlockSpec(memory_space=pltpu.SMEM),pl.BlockSpec(memory_space=pltpu.VMEM)],
      out_specs=pl.BlockSpec(memory_space=pltpu.VMEM),
      scratch_shapes=[pltpu.VMEM((256,2,16,128),jnp.float32),pltpu.VMEM((256,2,16,128),jnp.float32),pltpu.VMEM((256,2,16,128),jnp.float32),pltpu.VMEM((256,2,16,128),jnp.float32),pltpu.VMEM((4,2,G*8,128),jnp.float32)],
      compiler_params=pltpu.CompilerParams(vmem_limit_bytes=30<<20))(slots.reshape(-1),count,tab.reshape(2,256,16,128))

def lag_rows():
    k=np.arange(512)[:,None]+60; l=np.arange(2001)[None]-1000+S
    a=((k*l)%S)*(2*math.pi/S); s=1/math.sqrt(8192)
    t=np.stack([(np.cos(a)*s).reshape(8,64,2001),(-np.sin(a)*s).reshape(8,64,2001)],1)
    return t.reshape(1024,2001).astype(ml_dtypes.bfloat16)
def lag_kernel(x_ref,t_ref,o_ref):
    x=jnp.concatenate([x_ref[h,w] for h in range(2) for w in range(4)],1)
    o_ref[...]=jnp.dot(x,t_ref[...],preferred_element_type=jnp.float32)
def lag(x,tab):
    return pl.pallas_call(lag_kernel,out_shape=jax.ShapeDtypeStruct((512,2001),jnp.float32),grid=(4,),
      in_specs=[pl.BlockSpec((2,4,128,128),lambda i:(0,0,i,0)),pl.BlockSpec((1024,2001),lambda i:(0,0))],
      out_specs=pl.BlockSpec((128,2001),lambda i:(i,0)),
      compiler_params=pltpu.CompilerParams(vmem_limit_bytes=40<<20))(x,tab)

def place():
    w=lax.axis_index("win"); m=lax.axis_index("chan")
    return w,m//8,(m//2)%4,m%2
def greet(devs):
    bar=pltpu.get_barrier_semaphore()
    for d in devs: pl.semaphore_signal(bar,inc=1,device_id=d,device_id_type=MESH)
    pl.semaphore_wait(bar,len(devs))
def route(fr,wh,o_ref,xr,xf,ff,dd,gg,ra,rb,sx,rx,s1,r1,s2,r2,ls):
    w,y,z,c=place()
    dev=lambda p:(w,p[0]*8+p[1]*2+p[2])
    me=y*8+z*2+c
    peers=[((y+d)%4,z,(c+e)%2) for d in (1,2,3) for e in (0,1)]+[(y,(z+d)%4,(c+e)%2) for d in range(4) for e in range(2) if (d,e)!=(0,0)]
    greet([((w+d)%4,me) for d in (1,2,3)]+[dev(p) for p in peers])
    px={}
    for h in range(2):
        for i,d in enumerate((2,1,3)):
            t=(w+d)%4
            cp=pltpu.make_async_remote_copy(src_ref=wh.at[h,t],dst_ref=xr.at[h,w],send_sem=sx.at[h,i],recv_sem=rx.at[h,i],device_id=(t,me),device_id_type=MESH)
            cp.start(); px[h,i]=cp
    own=pltpu.make_async_copy(wh.at[:,w],xr.at[:,w],ls.at[10]); own.start(); own.wait()
    p1=[]
    for h in range(2):
        for i in range(3): px[h,i].wait()
        for s in range(4):
            xf[s]=xr[h,s].astype(jnp.float32)
        for s in range(4):
            for i in range(4):
                ff[pl.ds(4*s+i,64,stride=16)]=xf[s,pl.ds(i,64,stride=4)]
        dd[h]=ff[...].astype(jnp.bfloat16).reshape(64,16,128)
        def pick(o,_):
            for j in range(8):
                gg[h,o//8,(o//2)%4,o%2,pl.ds(16*j,16)]=dd[h,fr[o*8+j]]
            return 0
        lax.fori_loop(0,32,pick,0)
        row=[]
        for i,d in enumerate((2,1,3)):
            yy=(y+d)%4; zz=(z+d)%4
            if h==0: cp=pltpu.make_async_remote_copy(src_ref=gg.at[0,yy],dst_ref=ra.at[y],send_sem=s1.at[0,i],recv_sem=r1.at[0,i],device_id=dev((yy,z,c)),device_id_type=MESH)
            else: cp=pltpu.make_async_remote_copy(src_ref=gg.at[1,:,zz],dst_ref=rb.at[z],send_sem=s1.at[1,i],recv_sem=r1.at[1,i],device_id=dev((y,zz,c)),device_id_type=MESH)
            cp.start(); row.append(cp)
        p1.append(row)
    la=pltpu.make_async_copy(gg.at[0,y],ra.at[y],ls.at[0]); la.start()
    lb=pltpu.make_async_copy(gg.at[1,:,z],rb.at[z],ls.at[1]); lb.start()
    la.wait(); lb.wait()
    p2=[]
    def send2(k):
        d=(0,2,1,3)[k]
        ys=(y-d)%4; zs=(z-d)%4
        j=0
        for dz in (2,1,3,0):
            for dc in (1,0):
                zz=(z+dz)%4; yy=(y+dz)%4; cc=(c+dc)%2
                if (dz,dc)==(0,0):
                    l1=pltpu.make_async_copy(ra.at[ys,z,c],o_ref.at[0,ys,z,c],ls.at[2+2*k]); l1.start()
                    l2=pltpu.make_async_copy(rb.at[zs,y,c],o_ref.at[1,y,zs,c],ls.at[3+2*k]); l2.start()
                    p2.append((l1,l2)); continue
                ca=pltpu.make_async_remote_copy(src_ref=ra.at[ys,zz,cc],dst_ref=o_ref.at[0,ys,z,c],send_sem=s2.at[0,k,j],recv_sem=r2.at[0,k,j],device_id=dev((y,zz,cc)),device_id_type=MESH); ca.start()
                cb=pltpu.make_async_remote_copy(src_ref=rb.at[zs,yy,cc],dst_ref=o_ref.at[1,y,zs,c],send_sem=s2.at[1,k,j],recv_sem=r2.at[1,k,j],device_id=dev((yy,z,cc)),device_id_type=MESH); cb.start()
                p2.append((ca,cb)); j+=1
    send2(0)
    for i in range(3):
        p1[0][i].wait(); p1[1][i].wait(); send2(i+1)
    for a,b in p2: a.wait(); b.wait()
def exchange(fr,wh):
    B=jnp.bfloat16; D=pltpu.SemaphoreType.DMA
    return pl.pallas_call(route,out_shape=jax.ShapeDtypeStruct((2,4,4,2,128,128),B),
      in_specs=[pl.BlockSpec(memory_space=pltpu.SMEM),pl.BlockSpec(memory_space=pltpu.VMEM)],out_specs=pl.BlockSpec(memory_space=pltpu.VMEM),
      scratch_shapes=[pltpu.VMEM((2,4,256,128),B),pltpu.VMEM((4,256,128),jnp.float32),pltpu.VMEM((1024,128),jnp.float32),pltpu.VMEM((2,64,16,128),B),
        pltpu.VMEM((2,4,4,2,128,128),B),pltpu.VMEM((4,4,2,128,128),B),pltpu.VMEM((4,4,2,128,128),B),
        D((2,3)),D((2,3)),D((2,3)),D((2,3)),D((2,4,7)),D((2,4,7)),D((11,))],
      compiler_params=pltpu.CompilerParams(collective_id=1,has_side_effects=True,vmem_limit_bytes=40<<20))(fr,wh)
def swap(x_ref,o_ref,ss,rs,ls):
    w,y,z,c=place(); me=y*8+z*2+c
    greet([((w+d)%4,me) for d in (1,2,3)])
    cps=[]
    for i,d in enumerate((2,1,3)):
        t=(w+d)%4
        cp=pltpu.make_async_remote_copy(src_ref=x_ref.at[:,t],dst_ref=o_ref.at[:,w],send_sem=ss.at[i],recv_sem=rs.at[i],device_id=(t,me),device_id_type=MESH)
        cp.start(); cps.append(cp)
    own=pltpu.make_async_copy(x_ref.at[:,w],o_ref.at[:,w],ls); own.start(); own.wait()
    for cp in cps: cp.wait()
def hand_over(x):
    D=pltpu.SemaphoreType.DMA
    return pl.pallas_call(swap,out_shape=jax.ShapeDtypeStruct(x.shape,x.dtype),
      in_specs=[pl.BlockSpec(memory_space=pltpu.VMEM)],out_specs=pl.BlockSpec(memory_space=pltpu.VMEM),
      scratch_shapes=[D((3,)),D((3,)),D],
      compiler_params=pltpu.CompilerParams(collective_id=2,has_side_effects=True,vmem_limit_bytes=20<<20))(x)

def body(traces,fetch_rows,pair_slots,tile_count):
    wh=dft(traces,jnp.asarray(quarter_table()),jnp.asarray(turn_rows()))
    fr=lax.dynamic_index_in_dim(fetch_rows,lax.axis_index("chan"),1,keepdims=False).reshape(-1)
    tab=exchange(fr,wh.reshape(2,4,256,128))
    part=cross(pair_slots,tile_count,tab)
    full=hand_over(part)
    return lag(full,jnp.asarray(lag_rows())).reshape(16,32,2001)

def solution(mesh):
    return jax.shard_map(body,mesh=mesh,in_specs=(P("chan","win",None),P(),P("chan",None,None),P("chan")),
      out_specs=P("chan","win",None),check_vma=False)
```

```python
import functools
import math

import jax
import jax.numpy as jnp
import ml_dtypes
import numpy as np
from jax import lax
from jax.experimental import pallas as pl
from jax.experimental.pallas import tpu as pltpu
from jax.sharding import PartitionSpec as P

MESH=pl.DeviceIdType.MESH
S=14976
def quarter_table():
    s=np.arange(3840)[:,None]; k=np.arange(512)[None]+60
    a=((s*k)%S)*(2*math.pi/S)
    c=np.cos(a).reshape(3840,8,1,64); d=-np.sin(a).reshape(3840,8,1,64)
    return np.concatenate([c,d],2).reshape(3840,1024).astype(ml_dtypes.bfloat16)
def turn_rows():
    lane=np.arange(1024)%128; k=(np.arange(1024)//128)*64+lane%64; im=lane>=64
    s=np.where(k%2==0,1.,-1.)
    al=np.array([1,0,-1,0.])[k%4]
    be=np.where(im,np.array([0,-1,0,1.])[k%4],np.array([0,1,0,-1.])[k%4])
    return np.stack([s,al,be]+[s*0]*5).astype(np.float32)
FIRST=(0,30,59,88); COUNT=(30,29,29,29); SHIFT=(0,96,64,32)
def lag_rows():
    k=np.arange(512)[:,None]+60; l=np.arange(2001)[None]-1000+S
    a=((k*l)%S)*(2*math.pi/S); s=1/math.sqrt(8192)
    t=np.stack([(np.cos(a)*s).reshape(8,64,2001),(-np.sin(a)*s).reshape(8,64,2001)],1)
    return t.reshape(1024,2001).astype(ml_dtypes.bfloat16)
def lag_kernel(x_ref,t_ref,o_ref):
    x=jnp.concatenate([x_ref[h,w] for h in range(2) for w in range(4)],1)
    o_ref[...]=jnp.dot(x,t_ref[...],preferred_element_type=jnp.float32)
def lag(x,tab):
    return pl.pallas_call(lag_kernel,out_shape=jax.ShapeDtypeStruct((512,2001),jnp.float32),grid=(4,),
      in_specs=[pl.BlockSpec((2,4,128,128),lambda i:(0,0,i,0)),pl.BlockSpec((1024,2001),lambda i:(0,0))],
      out_specs=pl.BlockSpec((128,2001),lambda i:(i,0)),
      compiler_params=pltpu.CompilerParams(vmem_limit_bytes=40<<20))(x,tab)


F=jnp.float32
B=jnp.bfloat16
HOPS=(0,2,1,3)

def whitened(acc,turn,h,b):
    cs=slice(512*h+128*b,512*h+128*b+128); gs=slice(128*b,128*b+128)
    s,al,be=turn[0:1,cs],turn[1:2,cs],turn[2:3,cs]
    g0,g1,g2,g3=(acc[q,:,gs] for q in range(4))
    z=g0+s*g2+al*(g1+g3)+be*pltpu.roll(g1-g3,64,1)
    sq=z*z
    mag=jnp.sqrt(sq+pltpu.roll(sq,64,1))
    level=jnp.sum(mag,axis=1,keepdims=True)*(1/128)+1e-6
    return (z*(1.0/level)).astype(B)

def whole(fr,slots,count,x_ref,t_ref,turn,o_ref,xs,ts,acc,wh,xr,xf,ff,dd,gg,ra,rb,tab,a1,a2,r1,r2,sr,part,
          xsem,tsem,sx,rx,s1,q1,s2,q2,sp,rp,ls):
    w=lax.axis_index("win"); me=lax.axis_index("chan")
    y,z,c=me//8,(me//2)%4,me%2
    dev=lambda yy,zz,cc:(w,yy*8+zz*2+cc)
    def send(src,dst,ss,rs,to):
        cp=pltpu.make_async_remote_copy(src_ref=src,dst_ref=dst,send_sem=ss,recv_sem=rs,device_id=to,device_id_type=MESH)
        cp.start()
        return cp
    def move(src,dst,sem):
        cp=pltpu.make_async_copy(src,dst,sem)
        cp.start()
        return cp
    tc=[pltpu.make_async_copy(t_ref.at[h],ts.at[h],tsem.at[h]) for h in range(2)]
    xc=[pltpu.make_async_copy(x_ref.at[:,:,pl.ds(128*FIRST[q],128*COUNT[q])],xs.at[:,:,pl.ds(128*FIRST[q],128*COUNT[q])],xsem.at[q]) for q in range(4)]
    tc[0].start()
    for q in range(4): xc[q].start()
    tc[1].start()
    bar=pltpu.get_barrier_semaphore()
    peers=[((w+d)%4,me) for d in (1,2,3)]+[dev((y+d)%4,z,(c+e)%2) for d in (1,2,3) for e in (0,1)]
    peers+=[dev(y,(z+d)%4,(c+e)%2) for d in range(4) for e in range(2) if (d,e)!=(0,0)]
    for p in peers: pl.semaphore_signal(bar,inc=1,device_id=p,device_id_type=MESH)

    def dft(h,q):
        if h==0: xc[q].wait()
        a,n=128*FIRST[q],128*COUNT[q]
        acc[q]=jnp.dot(xs[:,:,a:a+n].reshape(256,n),ts[h,SHIFT[q]:SHIFT[q]+n,:],preferred_element_type=F)
    def whiten(h):
        for b in range(4): wh[h,b]=whitened(acc,turn,h,b)
        cps=[send(wh.at[h,(w+d)%4],xr.at[h,w],sx.at[h,i],rx.at[h,i],((w+d)%4,me)) for i,d in enumerate((2,1,3))]
        return cps+[move(wh.at[h,w],xr.at[h,w],ls.at[h])]
    def pick(h,cps):
        for cp in cps: cp.wait()
        for s in range(4): xf[s]=xr[h,s].astype(F)
        for s in range(4):
            for i in range(4): ff[pl.ds(4*s+i,64,stride=16)]=xf[s,pl.ds(i,64,stride=4)]
        dd[h]=ff[...].astype(B).reshape(64,16,128)
        def owner(o,_):
            for j in range(8):
                gg[h,j//4,o//8,(o//2)%4,o%2,pl.ds(16*(j%4),16)]=dd[h,fr[o*8+j]]
            return 0
        lax.fori_loop(0,32,owner,0)
    def second(h,k):
        ys,zs=(y-HOPS[k])%4,(z-HOPS[k])%4
        cps=[]; j=0
        for dz in (2,1,3,0):
            for dc in (1,0):
                zz,yy,cc=(z+dz)%4,(y+dz)%4,(c+dc)%2
                if (dz,dc)==(0,0):
                    cps.append(move(ra.at[h,ys,z,c],tab.at[h,ys,z,c,0],ls.at[6+8*h+2*k]))
                    cps.append(move(rb.at[h,zs,y,c],tab.at[h,y,zs,c,1],ls.at[7+8*h+2*k]))
                    continue
                cps.append(send(ra.at[h,ys,zz,cc],tab.at[h,ys,z,c,0],s2.at[h,0,k,j],q2.at[h,0,k,j],dev(y,zz,cc)))
                cps.append(send(rb.at[h,zs,yy,cc],tab.at[h,y,zs,c,1],s2.at[h,1,k,j],q2.at[h,1,k,j],dev(yy,z,cc)))
                j+=1
        return cps
    def first(h):
        cps=[]
        for i,d in enumerate(HOPS[1:]):
            yy,zz=(y+d)%4,(z+d)%4
            cps.append((send(gg.at[h,0,yy],ra.at[h,y],s1.at[h,0,i],q1.at[h,0,i],dev(yy,z,c)),
                        send(gg.at[h,1,:,zz],rb.at[h,z],s1.at[h,1,i],q1.at[h,1,i],dev(y,zz,c))))
        own=[move(gg.at[h,0,y],ra.at[h,y],ls.at[2+2*h]),move(gg.at[h,1,:,z],rb.at[h,z],ls.at[3+2*h])]
        for cp in own: cp.wait()
        return cps,second(h,0)
    def forward(h,cps):
        out=[]
        for k in range(3):
            for cp in cps[k]: cp.wait()
            out+=second(h,k+1)
        return out
    ri=lax.broadcasted_iota(jnp.int32,(128,128),0); ci=lax.broadcasted_iota(jnp.int32,(128,128),1)
    lo=ci<64
    unit=lambda m,v: jnp.where(m,v,0.0).astype(B)
    turns=jnp.concatenate([unit(ri==ci+jnp.where(lo,64,-64),jnp.where(lo,1.0,-1.0)),unit(ri==ci-jnp.where(lo,0,64),1.0),unit(ri==ci+jnp.where(lo,64,0),1.0)],1)
    def spread(h):
        def block(i,_):
            v=tab[h,i//4,i%4].reshape(256,128)
            v2=jnp.dot(v,turns,preferred_element_type=F)
            rows=pl.ds(i*16,16)
            a1[h,rows]=v.astype(F).reshape(16,16,128)
            for m,ref in enumerate((a2,r1,r2)): ref[h,rows]=v2[:,128*m:128*m+128].reshape(16,16,128)
            return 0
        lax.fori_loop(0,16,block,0)
    live=count[0]
    def cross(h,t):
        keep=jnp.where(t<live,1.0,0.0).astype(F)
        def reduce(g):
            v=[sr[g,pl.ds(j,32,stride=8)] for j in range(8)]
            v=((v[0]+v[1])+(v[2]+v[3]))+((v[4]+v[5])+(v[6]+v[7]))
            part[h,g,pl.ds(pl.multiple_of(t*32,32),32)]=(v*keep).astype(B)
        for g in range(4):
            for i in range(32):
                s=slots[t*256+g*32+i]; r=slots[t*256+128+g*32+i]
                v=a1[h,s]*r1[h,r]+a2[h,s]*r2[h,r]
                sr[g,pl.ds(8*i,8)]=v[:8]+v[8:]
            if g: reduce(g-1)
        reduce(3)
    def hand_over(h,n):
        def tile(t,_):
            cross(h,4*n+t)
            return 0
        lax.fori_loop(0,4,tile,0)
        rows=pl.ds(128*n,128)
        cps=[send(part.at[h,(w+d)%4,rows],o_ref.at[h,w,rows],sp.at[h,n,i],rp.at[h,n,i],((w+d)%4,me)) for i,d in enumerate((2,1,3))]
        return cps+[move(part.at[h,w,rows],o_ref.at[h,w,rows],ls.at[22+4*h+n])]

    tc[0].wait()
    for q in range(4): dft(0,q)
    for b in range(4): wh[0,b]=whitened(acc,turn,0,b)
    pl.semaphore_wait(bar,len(peers))
    px0=[send(wh.at[0,(w+d)%4],xr.at[0,w],sx.at[0,i],rx.at[0,i],((w+d)%4,me)) for i,d in enumerate((2,1,3))]
    px0.append(move(wh.at[0,w],xr.at[0,w],ls.at[0]))
    tc[1].wait()
    for q in range(3): dft(1,q)
    pick(0,px0)
    p1a,p2a=first(0)
    dft(1,3)
    px1=whiten(1)
    p2a+=forward(0,p1a)
    pick(1,px1)
    p1b,p2b=first(1)
    for cp in p2a: cp.wait()
    spread(0)
    p2b+=forward(1,p1b)
    last=[]
    for n in range(4): last+=hand_over(0,n)
    for cp in p2b: cp.wait()
    spread(1)
    for n in range(4): last+=hand_over(1,n)
    for cp in last: cp.wait()

def correlate(fr,slots,count,x,table,turn):
    D=pltpu.SemaphoreType.DMA; V=pltpu.VMEM
    smem=pl.BlockSpec(memory_space=pltpu.SMEM); far=pl.BlockSpec(memory_space=pl.ANY); near=pl.BlockSpec(memory_space=pltpu.VMEM)
    return pl.pallas_call(whole,out_shape=jax.ShapeDtypeStruct((2,4,512,128),B),
      in_specs=[smem,smem,smem,far,far,near],out_specs=near,
      scratch_shapes=[V((64,4,S),B),V((2,3840,512),B),V((4,256,512),F),V((2,4,256,128),B),V((2,4,256,128),B),V((4,256,128),F),V((1024,128),F),V((2,64,16,128),B),
        V((2,2,4,4,2,64,128),B),V((2,4,4,2,64,128),B),V((2,4,4,2,64,128),B),V((2,4,4,2,2,64,128),B)]+[V((2,256,16,128),F)]*4+[V((4,256,128),F),V((2,4,512,128),B),
        D((4,)),D((2,)),D((2,3)),D((2,3)),D((2,2,3)),D((2,2,3)),D((2,2,4,7)),D((2,2,4,7)),D((2,4,3)),D((2,4,3)),D((30,))],
      compiler_params=pltpu.CompilerParams(collective_id=1,has_side_effects=True,vmem_limit_bytes=58<<20))(fr,slots,count,x,table,turn)

def body(traces,fetch_rows,pair_slots,tile_count):
    fr=lax.dynamic_index_in_dim(fetch_rows,lax.axis_index("chan"),1,keepdims=False).reshape(-1)
    table=quarter_table()
    table=jnp.asarray(np.stack([table[:,:512],table[:,512:]]))
    full=correlate(fr,pair_slots.reshape(-1),tile_count,traces,table,jnp.asarray(turn_rows()))
    return lag(full,jnp.asarray(lag_rows())).reshape(16,32,2001)

def solution(mesh):
    return jax.shard_map(body,mesh=mesh,in_specs=(P("chan","win",None),P(),P("chan",None,None),P("chan")),
      out_specs=P("chan","win",None),check_vma=False)
```

```python
import functools
import math

import jax
import jax.numpy as jnp
import ml_dtypes
import numpy as np
from jax import lax
from jax.experimental import pallas as pl
from jax.experimental.pallas import tpu as pltpu
from jax.sharding import PartitionSpec as P

MESH=pl.DeviceIdType.MESH
S=14976
def quarter_table():
    s=np.arange(3840)[:,None]; k=np.arange(512)[None]+60
    a=((s*k)%S)*(2*math.pi/S)
    c=np.cos(a).reshape(3840,8,1,64); d=-np.sin(a).reshape(3840,8,1,64)
    return np.concatenate([c,d],2).reshape(3840,1024).astype(ml_dtypes.bfloat16)
FIRST=(0,30,59,88); COUNT=(30,29,29,29); SHIFT=(0,96,64,32)
def lag_rows():
    k=np.arange(512)[:,None]+60; l=np.arange(2001)[None]-1000+S
    a=((k*l)%S)*(2*math.pi/S); s=1/math.sqrt(8192)
    t=np.stack([(np.cos(a)*s).reshape(8,64,2001),(-np.sin(a)*s).reshape(8,64,2001)],1)
    return t.reshape(1024,2001).astype(ml_dtypes.bfloat16)
F=jnp.float32
B=jnp.bfloat16
HOPS=(0,2,1,3)

def lag_kernel(x_ref,t_ref,o_ref,buf,sem):
    cps=[]
    for i in range(4):
        rows=slice(128*i,128*i+128)
        x=jnp.concatenate([x_ref[h,w,rows] for h in range(2) for w in range(4)],1)
        buf[rows]=jnp.dot(x,t_ref[...],preferred_element_type=F)
        cp=pltpu.make_async_copy(buf.at[rows],o_ref.at[rows],sem.at[i])
        cp.start(); cps.append(cp)
    for cp in cps: cp.wait()
def lag(x,tab):
    near=pl.BlockSpec(memory_space=pltpu.VMEM)
    return pl.pallas_call(lag_kernel,out_shape=jax.ShapeDtypeStruct((512,2001),F),in_specs=[near,near],
      out_specs=pl.BlockSpec(memory_space=pl.ANY),scratch_shapes=[pltpu.VMEM((512,2001),F),pltpu.SemaphoreType.DMA((4,))],
      compiler_params=pltpu.CompilerParams(vmem_limit_bytes=20<<20))(x,tab)

def whole(lists,slots,count,x_ref,t_ref,o_ref,fr,xs,ts,acc,wh,xr,xf,ff,dd,gg,ra,rb,tab,a1,a2,r1,r2,sr,part,
          fsem,xsem,tsem,sx,rx,s1,q1,s2,q2,sp,rp,ls):
    w=lax.axis_index("win"); me=lax.axis_index("chan")
    y,z,c=me//8,(me//2)%4,me%2
    dev=lambda yy,zz,cc:(w,yy*8+zz*2+cc)
    def send(src,dst,ss,rs,to):
        cp=pltpu.make_async_remote_copy(src_ref=src,dst_ref=dst,send_sem=ss,recv_sem=rs,device_id=to,device_id_type=MESH)
        cp.start()
        return cp
    def move(src,dst,sem):
        cp=pltpu.make_async_copy(src,dst,sem)
        cp.start()
        return cp
    tc=[pltpu.make_async_copy(t_ref.at[h],ts.at[h],tsem.at[h]) for h in range(2)]
    xc=[pltpu.make_async_copy(x_ref.at[:,:,pl.ds(128*FIRST[q],128*COUNT[q])],xs.at[:,:,pl.ds(128*FIRST[q],128*COUNT[q])],xsem.at[q]) for q in range(4)]
    tc[0].start()
    for q in range(4): xc[q].start()
    fc=pltpu.make_async_copy(lists,fr,fsem)
    fc.start()
    tc[1].start()
    bar=pltpu.get_barrier_semaphore()
    peers=[((w+d)%4,me) for d in (1,2,3)]+[dev((y+d)%4,z,(c+e)%2) for d in (1,2,3) for e in (0,1)]
    peers+=[dev(y,(z+d)%4,(c+e)%2) for d in range(4) for e in range(2) if (d,e)!=(0,0)]
    for p in peers: pl.semaphore_signal(bar,inc=1,device_id=p,device_id_type=MESH)

    def dft(h,q):
        if h==0: xc[q].wait()
        a,n=128*FIRST[q],128*COUNT[q]
        acc[q]=jnp.dot(xs[:,:,a:a+n].reshape(256,n),ts[h,SHIFT[q]:SHIFT[q]+n,:],preferred_element_type=F)
    lane=lax.broadcasted_iota(jnp.int32,(1,128),1)
    four=lane%4
    sg=(1-2*(lane%2)).astype(F)
    al=jnp.where(four==0,1.0,jnp.where(four==2,-1.0,0.0)).astype(F)
    be=jnp.where(four==1,1.0,jnp.where(four==3,-1.0,0.0)).astype(F)*jnp.where(lane<64,1.0,-1.0).astype(F)
    def whiten(h):
        for b in range(4):
            g0,g1,g2,g3=(acc[q,:,128*b:128*b+128] for q in range(4))
            v=g0+sg*g2+al*(g1+g3)+be*pltpu.roll(g1-g3,64,1)
            sq=v*v
            sq=sq+pltpu.roll(sq,64,1)
            mag=sq*lax.rsqrt(jnp.maximum(sq,1e-30))
            level=jnp.sum(mag,axis=1,keepdims=True)*(1/128)+1e-6
            wh[h,b]=(v*(1.0/level)).astype(B)
    def spectra(h):
        return [send(wh.at[h,(w+d)%4],xr.at[h,w],sx.at[h,i],rx.at[h,i],((w+d)%4,me)) for i,d in enumerate((2,1,3))]
    def pick(h,cps):
        for cp in cps: cp.wait()
        for d in range(4):
            xf[d]=(xr if d else wh)[h,(w+d)%4].astype(F)
        for d in range(4):
            for i in range(4): ff[pl.ds(4*d+i,64,stride=16)]=xf[d,pl.ds(i,64,stride=4)]
        dd[h]=ff[...].astype(B).reshape(64,16,128)
        def owner(o,_):
            for j in range(8):
                gg[h,j//4,o//8,(o//2)%4,o%2,pl.ds(16*(j%4),16)]=dd[h,fr[o,j,me]]
            return 0
        lax.fori_loop(0,32,owner,0)
    def second(h,k):
        ys,zs=(y-HOPS[k])%4,(z-HOPS[k])%4
        cps=[]; j=0
        for dz in (2,1,3,0):
            for dc in (1,0):
                zz,yy,cc=(z+dz)%4,(y+dz)%4,(c+dc)%2
                fa=ra.at[h,ys,zz,cc] if k else gg.at[h,0,y,zz,cc]
                fb=rb.at[h,zs,yy,cc] if k else gg.at[h,1,yy,z,cc]
                if (dz,dc)==(0,0):
                    cps.append(move(fa,tab.at[h,ys,z,c,0],ls.at[6+8*h+2*k]))
                    cps.append(move(fb,tab.at[h,y,zs,c,1],ls.at[7+8*h+2*k]))
                    continue
                cps.append(send(fa,tab.at[h,ys,z,c,0],s2.at[h,0,k,j],q2.at[h,0,k,j],dev(y,zz,cc)))
                cps.append(send(fb,tab.at[h,y,zs,c,1],s2.at[h,1,k,j],q2.at[h,1,k,j],dev(yy,z,cc)))
                j+=1
        return cps
    def first(h):
        cps=[]
        for i,d in enumerate(HOPS[1:]):
            yy,zz=(y+d)%4,(z+d)%4
            cps.append((send(gg.at[h,0,yy],ra.at[h,y],s1.at[h,0,i],q1.at[h,0,i],dev(yy,z,c)),
                        send(gg.at[h,1,:,zz],rb.at[h,z],s1.at[h,1,i],q1.at[h,1,i],dev(y,zz,c))))
        return cps,second(h,0)
    def forward(h,cps):
        out=[]
        for k in range(3):
            for cp in cps[k]: cp.wait()
            out+=second(h,k+1)
        return out
    ri=lax.broadcasted_iota(jnp.int32,(128,128),0); ci=lax.broadcasted_iota(jnp.int32,(128,128),1)
    lo=ci<64
    unit=lambda m,v: jnp.where(m,v,0.0).astype(B)
    turns=jnp.concatenate([unit(ri==ci+jnp.where(lo,64,-64),jnp.where(lo,1.0,-1.0)),unit(ri==ci-jnp.where(lo,0,64),1.0),unit(ri==ci+jnp.where(lo,64,0),1.0)],1)
    def spread(h):
        def block(i,_):
            v=tab[h,i//4,i%4].reshape(256,128)
            v2=jnp.dot(v,turns,preferred_element_type=F)
            rows=pl.ds(i*16,16)
            a1[h,rows]=v.astype(F).reshape(16,16,128)
            for m,ref in enumerate((a2,r1,r2)): ref[h,rows]=v2[:,128*m:128*m+128].reshape(16,16,128)
            return 0
        lax.fori_loop(0,16,block,0)
    live=count[0]
    def cross(h,t):
        keep=jnp.where(t<live,1.0,0.0).astype(F)
        def reduce(g):
            v=[sr[g,pl.ds(j,32,stride=8)] for j in range(8)]
            v=((v[0]+v[1])+(v[2]+v[3]))+((v[4]+v[5])+(v[6]+v[7]))
            part[h,g,pl.ds(pl.multiple_of(t*32,32),32)]=(v*keep).astype(B)
        for g in range(4):
            for i in range(32):
                s=slots[t*256+g*32+i]; r=slots[t*256+128+g*32+i]
                v=a1[h,s]*r1[h,r]+a2[h,s]*r2[h,r]
                sr[g,pl.ds(8*i,8)]=v[:8]+v[8:]
            if g: reduce(g-1)
        reduce(3)
    def hand_over(h,n):
        def tile(t,_):
            cross(h,4*n+t)
            return 0
        lax.fori_loop(0,4,tile,0)
        rows=pl.ds(128*n,128)
        cps=[send(part.at[h,(w+d)%4,rows],o_ref.at[h,w,rows],sp.at[h,n,i],rp.at[h,n,i],((w+d)%4,me)) for i,d in enumerate((2,1,3))]
        return cps+[move(part.at[h,w,rows],o_ref.at[h,w,rows],ls.at[22+4*h+n])]

    tc[0].wait()
    for q in range(4): dft(0,q)
    whiten(0)
    pl.semaphore_wait(bar,len(peers))
    px0=spectra(0)
    tc[1].wait()
    for q in range(3): dft(1,q)
    fc.wait()
    pick(0,px0)
    p1a,p2a=first(0)
    dft(1,3)
    whiten(1)
    px1=spectra(1)
    p2a+=forward(0,p1a)
    pick(1,px1)
    p1b,p2b=first(1)
    for cp in p2a: cp.wait()
    spread(0)
    last=hand_over(0,0)
    p2b+=forward(1,p1b)
    for n in range(1,4): last+=hand_over(0,n)
    for cp in p2b: cp.wait()
    spread(1)
    for n in range(4): last+=hand_over(1,n)
    for cp in last: cp.wait()

def correlate(lists,slots,count,x,table):
    D=pltpu.SemaphoreType.DMA; V=pltpu.VMEM
    smem=pl.BlockSpec(memory_space=pltpu.SMEM); far=pl.BlockSpec(memory_space=pl.ANY); near=pl.BlockSpec(memory_space=pltpu.VMEM)
    return pl.pallas_call(whole,out_shape=jax.ShapeDtypeStruct((2,4,512,128),B),
      in_specs=[far,smem,smem,far,far],out_specs=near,
      scratch_shapes=[pltpu.SMEM((32,8,32),jnp.int32),V((64,4,S),B),V((2,3840,512),B),V((4,256,512),F),V((2,4,256,128),B),V((2,4,256,128),B),V((4,256,128),F),V((1024,128),F),V((2,64,16,128),B),
        V((2,2,4,4,2,64,128),B),V((2,4,4,2,64,128),B),V((2,4,4,2,64,128),B),V((2,4,4,2,2,64,128),B)]+[V((2,256,16,128),F)]*4+[V((4,256,128),F),V((2,4,512,128),B),
        D,D((4,)),D((2,)),D((2,3)),D((2,3)),D((2,2,3)),D((2,2,3)),D((2,2,4,7)),D((2,2,4,7)),D((2,4,3)),D((2,4,3)),D((30,))],
      compiler_params=pltpu.CompilerParams(collective_id=1,has_side_effects=True,vmem_limit_bytes=50<<20))(lists,slots,count,x,table)

def body(traces,fetch_rows,pair_slots,tile_count):
    table=quarter_table()
    table=jnp.asarray(np.stack([table[:,:512],table[:,512:]]))
    full=correlate(fetch_rows.transpose(0,2,1),pair_slots.reshape(-1),tile_count,traces,table)
    return lag(full,jnp.asarray(lag_rows())).reshape(16,32,2001)

def solution(mesh):
    return jax.shard_map(body,mesh=mesh,in_specs=(P("chan","win",None),P(),P("chan",None,None),P("chan")),
      out_specs=P("chan","win",None),check_vma=False)
```

```python
import functools
import math

import jax
import jax.numpy as jnp
import ml_dtypes
import numpy as np
from jax import lax
from jax.experimental import pallas as pl
from jax.experimental.pallas import tpu as pltpu
from jax.sharding import PartitionSpec as P

MESH=pl.DeviceIdType.MESH
S=14976
def quarter_table():
    s=np.arange(3840)[:,None]; k=np.arange(512)[None]+60
    a=((s*k)%S)*(2*math.pi/S)
    c=np.cos(a).reshape(3840,8,1,64); d=-np.sin(a).reshape(3840,8,1,64)
    return np.concatenate([c,d],2).reshape(3840,1024).astype(ml_dtypes.bfloat16)
FIRST=(0,30,59,88); COUNT=(30,29,29,29); SHIFT=(0,96,64,32)
def lag_rows():
    k=np.arange(512)[:,None]+60; l=np.arange(2001)[None]-1000+S
    a=((k*l)%S)*(2*math.pi/S); s=1/math.sqrt(8192)
    t=np.stack([(np.cos(a)*s).reshape(8,64,2001),(-np.sin(a)*s).reshape(8,64,2001)],1)
    return t.reshape(1024,2001).astype(ml_dtypes.bfloat16)
F=jnp.float32
B=jnp.bfloat16
HOPS=(0,2,1,3)
GROUPS=((0,4,8,12,16),(0,2,6,11,16))

def lag_kernel(x_ref,t_ref,o_ref,buf,sem):
    cps=[]
    for i in range(4):
        rows=slice(128*i,128*i+128)
        x=jnp.concatenate([x_ref[h,w,rows] for h in range(2) for w in range(4)],1)
        buf[rows]=jnp.dot(x,t_ref[...],preferred_element_type=F)
        cp=pltpu.make_async_copy(buf.at[rows],o_ref.at[rows],sem.at[i])
        cp.start(); cps.append(cp)
    for cp in cps: cp.wait()
def lag(x,tab):
    near=pl.BlockSpec(memory_space=pltpu.VMEM)
    return pl.pallas_call(lag_kernel,out_shape=jax.ShapeDtypeStruct((512,2001),F),in_specs=[near,near],
      out_specs=pl.BlockSpec(memory_space=pl.ANY),scratch_shapes=[pltpu.VMEM((512,2001),F),pltpu.SemaphoreType.DMA((4,))],
      compiler_params=pltpu.CompilerParams(vmem_limit_bytes=20<<20))(x,tab)

def whole(lists,slots,count,x_ref,t_ref,o_ref,fr,xs,ts,acc,wh,xr,xf,ff,dd,gg,ra,rb,tab,a1,a2,r1,r2,sr,part,
          fsem,xsem,tsem,sx,rx,s1,q1,s2,q2,sp,rp,ls):
    w=lax.axis_index("win"); me=lax.axis_index("chan")
    y,z,c=me//8,(me//2)%4,me%2
    dev=lambda yy,zz,cc:(w,yy*8+zz*2+cc)
    def send(src,dst,ss,rs,to):
        cp=pltpu.make_async_remote_copy(src_ref=src,dst_ref=dst,send_sem=ss,recv_sem=rs,device_id=to,device_id_type=MESH)
        cp.start()
        return cp
    def move(src,dst,sem):
        cp=pltpu.make_async_copy(src,dst,sem)
        cp.start()
        return cp
    tc=[pltpu.make_async_copy(t_ref.at[h],ts.at[h],tsem.at[h]) for h in range(2)]
    xc=[pltpu.make_async_copy(x_ref.at[:,:,pl.ds(128*FIRST[q],128*COUNT[q])],xs.at[:,:,pl.ds(128*FIRST[q],128*COUNT[q])],xsem.at[q]) for q in range(4)]
    tc[0].start()
    for q in range(4): xc[q].start()
    fc=pltpu.make_async_copy(lists,fr,fsem)
    fc.start()
    tc[1].start()
    bar=pltpu.get_barrier_semaphore()
    peers=[((w+d)%4,me) for d in (1,2,3)]+[dev((y+d)%4,z,(c+e)%2) for d in (1,2,3) for e in (0,1)]
    peers+=[dev(y,(z+d)%4,(c+e)%2) for d in range(4) for e in range(2) if (d,e)!=(0,0)]
    for p in peers: pl.semaphore_signal(bar,inc=1,device_id=p,device_id_type=MESH)

    def dft(h,q):
        if h==0: xc[q].wait()
        a,n=128*FIRST[q],128*COUNT[q]
        acc[q]=jnp.dot(xs[:,:,a:a+n].reshape(256,n),ts[h,SHIFT[q]:SHIFT[q]+n,:],preferred_element_type=F)
    lane=lax.broadcasted_iota(jnp.int32,(1,128),1)
    four=lane%4
    sg=(1-2*(lane%2)).astype(F)
    al=jnp.where(four==0,1.0,jnp.where(four==2,-1.0,0.0)).astype(F)
    be=jnp.where(four==1,1.0,jnp.where(four==3,-1.0,0.0)).astype(F)*jnp.where(lane<64,1.0,-1.0).astype(F)
    def whiten(h):
        for b in range(4):
            g0,g1,g2,g3=(acc[q,:,128*b:128*b+128] for q in range(4))
            v=g0+sg*g2+al*(g1+g3)+be*pltpu.roll(g1-g3,64,1)
            sq=v*v
            sq=sq+pltpu.roll(sq,64,1)
            mag=sq*lax.rsqrt(jnp.maximum(sq,1e-30))
            level=jnp.sum(mag,axis=1,keepdims=True)*(1/128)+1e-6
            wh[h,b]=(v*(1.0/level)).astype(B)
    def spectra(h):
        return [send(wh.at[h,(w+d)%4],xr.at[h,w],sx.at[h,i],rx.at[h,i],((w+d)%4,me)) for i,d in enumerate((2,1,3))]
    def pick(h,cps):
        for cp in cps: cp.wait()
        for d in range(4):
            xf[d]=(xr if d else wh)[h,(w+d)%4].astype(F)
        for d in range(4):
            for i in range(4): ff[pl.ds(4*d+i,64,stride=16)]=xf[d,pl.ds(i,64,stride=4)]
        dd[h]=ff[...].astype(B).reshape(64,16,128)
        def owner(o,_):
            for j in range(8):
                gg[h,j//4,o//8,(o//2)%4,o%2,pl.ds(16*(j%4),16)]=dd[h,fr[o,j,me]]
            return 0
        lax.fori_loop(0,32,owner,0)
    def second(h,k):
        ys,zs=(y-HOPS[k])%4,(z-HOPS[k])%4
        cps=[]; j=0
        for dz in (2,1,3,0):
            for dc in (1,0):
                zz,yy,cc=(z+dz)%4,(y+dz)%4,(c+dc)%2
                fa=ra.at[h,ys,zz,cc] if k else gg.at[h,0,y,zz,cc]
                fb=rb.at[h,zs,yy,cc] if k else gg.at[h,1,yy,z,cc]
                if (dz,dc)==(0,0):
                    cps.append(move(fa,tab.at[h,ys,z,c,0],ls.at[6+8*h+2*k]))
                    cps.append(move(fb,tab.at[h,y,zs,c,1],ls.at[7+8*h+2*k]))
                    continue
                cps.append(send(fa,tab.at[h,ys,z,c,0],s2.at[h,0,k,j],q2.at[h,0,k,j],dev(y,zz,cc)))
                cps.append(send(fb,tab.at[h,y,zs,c,1],s2.at[h,1,k,j],q2.at[h,1,k,j],dev(yy,z,cc)))
                j+=1
        return cps
    def first(h):
        cps=[]
        for i,d in enumerate(HOPS[1:]):
            yy,zz=(y+d)%4,(z+d)%4
            cps.append((send(gg.at[h,0,yy],ra.at[h,y],s1.at[h,0,i],q1.at[h,0,i],dev(yy,z,c)),
                        send(gg.at[h,1,:,zz],rb.at[h,z],s1.at[h,1,i],q1.at[h,1,i],dev(y,zz,c))))
        return cps,second(h,0)
    def forward(h,cps,hops=range(3)):
        out=[]
        for k in hops:
            for cp in cps[k]: cp.wait()
            out+=second(h,k+1)
        return out
    ri=lax.broadcasted_iota(jnp.int32,(128,128),0); ci=lax.broadcasted_iota(jnp.int32,(128,128),1)
    lo=ci<64
    unit=lambda m,v: jnp.where(m,v,0.0).astype(B)
    turns=jnp.concatenate([unit(ri==ci+jnp.where(lo,64,-64),jnp.where(lo,1.0,-1.0)),unit(ri==ci-jnp.where(lo,0,64),1.0),unit(ri==ci+jnp.where(lo,64,0),1.0)],1)
    def spread(h,cps):
        for k in range(4):
            for cp in cps[16*k:16*k+16]: cp.wait()
            ys,zs=(y-HOPS[k])%4,(z-HOPS[k])%4
            def block(i,_):
                for r in range(2):
                    yy,zz=(ys,i) if r==0 else (i,zs)
                    v=tab[h,yy,zz,:,r].reshape(128,128)
                    v2=jnp.dot(v,turns,preferred_element_type=F)
                    parts=[v.astype(F)]+[v2[:,128*m:128*m+128] for m in range(3)]
                    for cc in range(2):
                        rows=pl.ds((yy*4+zz)*16+8*cc+4*r,4)
                        for ref,u in zip((a1,a2,r1,r2),parts): ref[h,rows]=u[64*cc:64*cc+64].reshape(4,16,128)
                return 0
            lax.fori_loop(0,4,block,0)
    live=count[0]
    def cross(h,t):
        keep=jnp.where(t<live,1.0,0.0).astype(F)
        def reduce(g):
            v=[sr[g,pl.ds(j,32,stride=8)] for j in range(8)]
            v=((v[0]+v[1])+(v[2]+v[3]))+((v[4]+v[5])+(v[6]+v[7]))
            part[h,g,pl.ds(pl.multiple_of(t*32,32),32)]=(v*keep).astype(B)
        for g in range(4):
            for i in range(32):
                s=slots[t*256+g*32+i]; r=slots[t*256+128+g*32+i]
                v=a1[h,s]*r1[h,r]+a2[h,s]*r2[h,r]
                sr[g,pl.ds(8*i,8)]=v[:8]+v[8:]
            if g: reduce(g-1)
        reduce(3)
    def hand_over(h,n):
        t0,t1=GROUPS[h][n:n+2]
        def tile(t,_):
            cross(h,t)
            return 0
        lax.fori_loop(t0,t1,tile,0)
        rows=pl.ds(32*t0,32*(t1-t0))
        cps=[send(part.at[h,(w+d)%4,rows],o_ref.at[h,w,rows],sp.at[h,n,i],rp.at[h,n,i],((w+d)%4,me)) for i,d in enumerate((2,1,3))]
        return cps+[move(part.at[h,w,rows],o_ref.at[h,w,rows],ls.at[22+4*h+n])]

    tc[0].wait()
    for q in range(4): dft(0,q)
    whiten(0)
    pl.semaphore_wait(bar,len(peers))
    px0=spectra(0)
    tc[1].wait()
    for q in range(3): dft(1,q)
    fc.wait()
    pick(0,px0)
    p1a,p2a=first(0)
    dft(1,3)
    whiten(1)
    px1=spectra(1)
    p2a+=forward(0,p1a)
    pick(1,px1)
    p1b,p2b=first(1)
    spread(0,p2a)
    last=hand_over(0,0)
    p2b+=forward(1,p1b,(0,))
    last+=hand_over(0,1)
    p2b+=forward(1,p1b,(1,2))
    for n in range(2,4): last+=hand_over(0,n)
    spread(1,p2b)
    for n in range(4): last+=hand_over(1,n)
    for cp in last: cp.wait()

def correlate(lists,slots,count,x,table):
    D=pltpu.SemaphoreType.DMA; V=pltpu.VMEM
    smem=pl.BlockSpec(memory_space=pltpu.SMEM); far=pl.BlockSpec(memory_space=pl.ANY); near=pl.BlockSpec(memory_space=pltpu.VMEM)
    return pl.pallas_call(whole,out_shape=jax.ShapeDtypeStruct((2,4,512,128),B),
      in_specs=[far,smem,smem,far,far],out_specs=near,
      scratch_shapes=[pltpu.SMEM((32,8,32),jnp.int32),V((64,4,S),B),V((2,3840,512),B),V((4,256,512),F),V((2,4,256,128),B),V((2,4,256,128),B),V((4,256,128),F),V((1024,128),F),V((2,64,16,128),B),
        V((2,2,4,4,2,64,128),B),V((2,4,4,2,64,128),B),V((2,4,4,2,64,128),B),V((2,4,4,2,2,64,128),B)]+[V((2,256,16,128),F)]*4+[V((4,256,128),F),V((2,4,512,128),B),
        D,D((4,)),D((2,)),D((2,3)),D((2,3)),D((2,2,3)),D((2,2,3)),D((2,2,4,7)),D((2,2,4,7)),D((2,4,3)),D((2,4,3)),D((30,))],
      compiler_params=pltpu.CompilerParams(collective_id=1,has_side_effects=True,vmem_limit_bytes=50<<20))(lists,slots,count,x,table)

def body(traces,fetch_rows,pair_slots,tile_count):
    table=quarter_table()
    table=jnp.asarray(np.stack([table[:,:512],table[:,512:]]))
    full=correlate(fetch_rows.transpose(0,2,1),pair_slots.reshape(-1),tile_count,traces,table)
    return lag(full,jnp.asarray(lag_rows())).reshape(16,32,2001)

def solution(mesh):
    return jax.shard_map(body,mesh=mesh,in_specs=(P("chan","win",None),P(),P("chan",None,None),P("chan")),
      out_specs=P("chan","win",None),check_vma=False)
```

```python
import functools
import math

import jax
import jax.numpy as jnp
import ml_dtypes
import numpy as np
from jax import lax
from jax.experimental import pallas as pl
from jax.experimental.pallas import tpu as pltpu
from jax.sharding import PartitionSpec as P

MESH=pl.DeviceIdType.MESH
S=14976
def quarter_table():
    s=np.arange(3840)[:,None]; k=np.arange(512)[None]+60
    a=((s*k)%S)*(2*math.pi/S)
    c=np.cos(a).reshape(3840,8,1,64); d=-np.sin(a).reshape(3840,8,1,64)
    return np.concatenate([c,d],2).reshape(3840,1024).astype(ml_dtypes.bfloat16)
FIRST=(0,30,59,88); COUNT=(30,29,29,29); SHIFT=(0,96,64,32)
def lag_rows():
    k=np.arange(512)[:,None]+60; l=np.arange(2001)[None]-1000+S
    a=((k*l)%S)*(2*math.pi/S); s=1/math.sqrt(8192)
    t=np.stack([(np.cos(a)*s).reshape(8,64,2001),(-np.sin(a)*s).reshape(8,64,2001)],1)
    return t.reshape(1024,2001).astype(ml_dtypes.bfloat16)
F=jnp.float32
B=jnp.bfloat16
HOPS=(0,2,1,3)
GROUPS=((0,4,8,12,16),(0,2,6,11,16))

def lag_kernel(x_ref,t_ref,o_ref,buf,sem):
    cps=[]
    for i in range(4):
        rows=slice(128*i,128*i+128)
        x=jnp.concatenate([x_ref[h,w,rows] for h in range(2) for w in range(4)],1)
        buf[rows]=jnp.dot(x,t_ref[...],preferred_element_type=F)
        cp=pltpu.make_async_copy(buf.at[rows],o_ref.at[rows],sem.at[i])
        cp.start(); cps.append(cp)
    for cp in cps: cp.wait()
def lag(x,tab):
    near=pl.BlockSpec(memory_space=pltpu.VMEM)
    return pl.pallas_call(lag_kernel,out_shape=jax.ShapeDtypeStruct((512,2001),F),in_specs=[near,near],
      out_specs=pl.BlockSpec(memory_space=pl.ANY),scratch_shapes=[pltpu.VMEM((512,2001),F),pltpu.SemaphoreType.DMA((4,))],
      compiler_params=pltpu.CompilerParams(vmem_limit_bytes=20<<20))(x,tab)

def whole(lists,slots,count,x_ref,t_ref,o_ref,fr,xs,ts,acc,wh,xr,xf,ff,dd,gg,ra,rb,tab,a1,a2,r1,r2,sr,part,
          fsem,xsem,tsem,sx,rx,s1,q1,s2,q2,sp,rp,ls):
    w=lax.axis_index("win"); me=lax.axis_index("chan")
    y,z,c=me//8,(me//2)%4,me%2
    dev=lambda yy,zz,cc:(w,yy*8+zz*2+cc)
    def send(src,dst,ss,rs,to):
        cp=pltpu.make_async_remote_copy(src_ref=src,dst_ref=dst,send_sem=ss,recv_sem=rs,device_id=to,device_id_type=MESH)
        cp.start()
        return cp
    def move(src,dst,sem):
        cp=pltpu.make_async_copy(src,dst,sem)
        cp.start()
        return cp
    tc=[pltpu.make_async_copy(t_ref.at[h],ts.at[h],tsem.at[h]) for h in range(2)]
    xc=[pltpu.make_async_copy(x_ref.at[:,:,pl.ds(128*FIRST[q],128*COUNT[q])],xs.at[:,:,pl.ds(128*FIRST[q],128*COUNT[q])],xsem.at[q]) for q in range(4)]
    tc[0].start()
    for q in range(4): xc[q].start()
    fc=pltpu.make_async_copy(lists,fr,fsem)
    fc.start()
    tc[1].start()
    bar=pltpu.get_barrier_semaphore()
    peers=[((w+d)%4,me) for d in (1,2,3)]+[dev((y+d)%4,z,(c+e)%2) for d in (1,2,3) for e in (0,1)]
    peers+=[dev(y,(z+d)%4,(c+e)%2) for d in range(4) for e in range(2) if (d,e)!=(0,0)]
    for p in peers: pl.semaphore_signal(bar,inc=1,device_id=p,device_id_type=MESH)

    def dft(h,q):
        if h==0: xc[q].wait()
        a,n=128*FIRST[q],128*COUNT[q]
        acc[q]=jnp.dot(xs[:,:,a:a+n].reshape(256,n),ts[h,SHIFT[q]:SHIFT[q]+n,:],preferred_element_type=F)
    lane=lax.broadcasted_iota(jnp.int32,(1,128),1)
    four=lane%4
    sg=(1-2*(lane%2)).astype(F)
    al=jnp.where(four==0,1.0,jnp.where(four==2,-1.0,0.0)).astype(F)
    be=jnp.where(four==1,1.0,jnp.where(four==3,-1.0,0.0)).astype(F)*jnp.where(lane<64,1.0,-1.0).astype(F)
    def whiten(h):
        for b in range(4):
            g0,g1,g2,g3=(acc[q,:,128*b:128*b+128] for q in range(4))
            v=g0+sg*g2+al*(g1+g3)+be*pltpu.roll(g1-g3,64,1)
            sq=v*v
            sq=sq+pltpu.roll(sq,64,1)
            mag=sq*lax.rsqrt(jnp.maximum(sq,1e-30))
            level=jnp.sum(mag,axis=1,keepdims=True)*(1/128)+1e-6
            wh[h,b]=(v*(1.0/level)).astype(B)
    def spectra(h):
        return [send(wh.at[h,(w+d)%4],xr.at[h,w],sx.at[h,i],rx.at[h,i],((w+d)%4,me)) for i,d in enumerate((2,1,3))]
    def pick(h,cps):
        for cp in cps: cp.wait()
        for d in range(4):
            xf[d]=(xr if d else wh)[h,(w+d)%4].astype(F)
        for d in range(4):
            for i in range(4): ff[pl.ds(4*d+i,64,stride=16)]=xf[d,pl.ds(i,64,stride=4)]
        dd[h]=ff[...].astype(B).reshape(64,16,128)
        def owner(o,_):
            for j in range(8):
                gg[h,j//4,o//8,(o//2)%4,o%2,pl.ds(16*(j%4),16)]=dd[h,fr[o,j,me]]
            return 0
        lax.fori_loop(0,32,owner,0)
    def second(h,k):
        ys,zs=(y-HOPS[k])%4,(z-HOPS[k])%4
        cps=[]; j=0
        for dz in (2,1,3,0):
            for dc in (1,0):
                zz,yy,cc=(z+dz)%4,(y+dz)%4,(c+dc)%2
                fa=ra.at[h,ys,zz,cc] if k else gg.at[h,0,y,zz,cc]
                fb=rb.at[h,zs,yy,cc] if k else gg.at[h,1,yy,z,cc]
                if (dz,dc)==(0,0):
                    cps.append(move(fa,tab.at[h,ys,z,c,0],ls.at[6+8*h+2*k]))
                    cps.append(move(fb,tab.at[h,y,zs,c,1],ls.at[7+8*h+2*k]))
                    continue
                cps.append(send(fa,tab.at[h,ys,z,c,0],s2.at[h,0,k,j],q2.at[h,0,k,j],dev(y,zz,cc)))
                cps.append(send(fb,tab.at[h,y,zs,c,1],s2.at[h,1,k,j],q2.at[h,1,k,j],dev(yy,z,cc)))
                j+=1
        return cps
    def first(h):
        cps=[]
        for i,d in enumerate(HOPS[1:]):
            yy,zz=(y+d)%4,(z+d)%4
            cps.append((send(gg.at[h,0,yy],ra.at[h,y],s1.at[h,0,i],q1.at[h,0,i],dev(yy,z,c)),
                        send(gg.at[h,1,:,zz],rb.at[h,z],s1.at[h,1,i],q1.at[h,1,i],dev(y,zz,c))))
        return cps,second(h,0)
    def forward(h,cps,hops=range(3)):
        out=[]
        for k in hops:
            for cp in cps[k]: cp.wait()
            out+=second(h,k+1)
        return out
    ri=lax.broadcasted_iota(jnp.int32,(128,128),0); ci=lax.broadcasted_iota(jnp.int32,(128,128),1)
    lo=ci<64
    unit=lambda m,v: jnp.where(m,v,0.0).astype(B)
    turns=jnp.concatenate([unit(ri==ci+jnp.where(lo,64,-64),jnp.where(lo,1.0,-1.0)),unit(ri==ci-jnp.where(lo,0,64),1.0),unit(ri==ci+jnp.where(lo,64,0),1.0)],1)
    def spread(h,cps):
        for k in range(4):
            for cp in cps[16*k:16*k+16]: cp.wait()
            ys,zs=(y-HOPS[k])%4,(z-HOPS[k])%4
            def block(i,_):
                for r in range(2):
                    yy,zz=(ys,i) if r==0 else (i,zs)
                    v=tab[h,yy,zz,:,r].reshape(128,128)
                    v2=jnp.dot(v,turns,preferred_element_type=F)
                    parts=[v.astype(F)]+[v2[:,128*m:128*m+128] for m in range(3)]
                    for cc in range(2):
                        rows=pl.ds((yy*4+zz)*16+8*cc+4*r,4)
                        for ref,u in zip((a1,a2,r1,r2),parts): ref[h,rows]=u[64*cc:64*cc+64].reshape(4,16,128)
                return 0
            lax.fori_loop(0,4,block,0)
    live=count[0]
    def cross(h,t):
        keep=jnp.where(t<live,1.0,0.0).astype(F)
        def reduce(g):
            v=[sr[g,pl.ds(j,32,stride=8)] for j in range(8)]
            v=((v[0]+v[1])+(v[2]+v[3]))+((v[4]+v[5])+(v[6]+v[7]))
            part[h,g,pl.ds(pl.multiple_of(t*32,32),32)]=(v*keep).astype(B)
        for g in range(4):
            for i in range(32):
                s=slots[t*256+g*32+i]; r=slots[t*256+128+g*32+i]
                v=a1[h,s]*r1[h,r]+a2[h,s]*r2[h,r]
                sr[g,pl.ds(8*i,8)]=v[:8]+v[8:]
            if g: reduce(g-1)
        reduce(3)
    def hand_over(h,n):
        t0,t1=GROUPS[h][n:n+2]
        def tile(t,_):
            cross(h,t)
            return 0
        lax.fori_loop(t0,t1,tile,0)
        rows=pl.ds(32*t0,32*(t1-t0))
        cps=[send(part.at[h,(w+d)%4,rows],o_ref.at[h,w,rows],sp.at[h,n,i],rp.at[h,n,i],((w+d)%4,me)) for i,d in enumerate((2,1,3))]
        return cps+[move(part.at[h,w,rows],o_ref.at[h,w,rows],ls.at[22+4*h+n])]

    tc[0].wait()
    for q in range(4): dft(0,q)
    whiten(0)
    pl.semaphore_wait(bar,len(peers))
    px0=spectra(0)
    tc[1].wait()
    for q in range(4): dft(1,q)
    fc.wait()
    pick(0,px0)
    p1a,p2a=first(0)
    whiten(1)
    px1=spectra(1)
    p2a+=forward(0,p1a)
    pick(1,px1)
    p1b,p2b=first(1)
    spread(0,p2a)
    last=hand_over(0,0)
    p2b+=forward(1,p1b,(0,))
    last+=hand_over(0,1)
    p2b+=forward(1,p1b,(1,2))
    for n in range(2,4): last+=hand_over(0,n)
    spread(1,p2b)
    for n in range(4): last+=hand_over(1,n)
    for cp in last: cp.wait()

def correlate(lists,slots,count,x,table):
    D=pltpu.SemaphoreType.DMA; V=pltpu.VMEM
    smem=pl.BlockSpec(memory_space=pltpu.SMEM); far=pl.BlockSpec(memory_space=pl.ANY); near=pl.BlockSpec(memory_space=pltpu.VMEM)
    return pl.pallas_call(whole,out_shape=jax.ShapeDtypeStruct((2,4,512,128),B),
      in_specs=[far,smem,smem,far,far],out_specs=near,
      scratch_shapes=[pltpu.SMEM((32,8,32),jnp.int32),V((64,4,S),B),V((2,3840,512),B),V((4,256,512),F),V((2,4,256,128),B),V((2,4,256,128),B),V((4,256,128),F),V((1024,128),F),V((2,64,16,128),B),
        V((2,2,4,4,2,64,128),B),V((2,4,4,2,64,128),B),V((2,4,4,2,64,128),B),V((2,4,4,2,2,64,128),B)]+[V((2,256,16,128),F)]*4+[V((4,256,128),F),V((2,4,512,128),B),
        D,D((4,)),D((2,)),D((2,3)),D((2,3)),D((2,2,3)),D((2,2,3)),D((2,2,4,7)),D((2,2,4,7)),D((2,4,3)),D((2,4,3)),D((30,))],
      compiler_params=pltpu.CompilerParams(collective_id=1,has_side_effects=True,vmem_limit_bytes=50<<20))(lists,slots,count,x,table)

def body(traces,fetch_rows,pair_slots,tile_count):
    table=quarter_table()
    table=jnp.asarray(np.stack([table[:,:512],table[:,512:]]))
    full=correlate(fetch_rows.transpose(0,2,1),pair_slots.reshape(-1),tile_count,traces,table)
    return lag(full,jnp.asarray(lag_rows())).reshape(16,32,2001)

def solution(mesh):
    return jax.shard_map(body,mesh=mesh,in_specs=(P("chan","win",None),P(),P("chan",None,None),P("chan")),
      out_specs=P("chan","win",None),check_vma=False)
```
